32 devices in a mesh: pipe: 4 (over z), dp: 2 (over x), tensor: 4 (over y, core).
Axes of the slice: x: 2, y: 2, z: 4, core: 2. Of those that a mesh axis runs over, the one named last changes fastest.
Arguments:
- tokens: bfloat16 [512, 12288], P(('pipe', 'tensor'), 'dp'), may hold values from -6 to 6
- out_grad: bfloat16 [512, 12288], P(('pipe', 'tensor'), 'dp'), may hold values from -3 to 3
- w_in: bfloat16 [12288, 24576], P('dp', ('pipe', 'tensor')), may hold values from -0.0546875 to 0.0546875
- b_in: float32 [24576], P(('pipe', 'tensor')), may hold values from -3 to 3
- w_out: bfloat16 [24576, 12288], P(('pipe', 'tensor'), 'dp'), may hold values from -0.0390625 to 0.0390625
Outputs:
- in_grad: bfloat16 [512, 12288], P(('pipe', 'tensor'), 'dp')
- w_in_grad: bfloat16 [12288, 24576], P('dp', ('pipe', 'tensor'))
- w_out_grad: bfloat16 [24576, 12288], P(('pipe', 'tensor'), 'dp')
- b_in_grad: float32 [24576], P(('pipe', 'tensor'))
The draws below stay inside these ranges and needn't reach their ends.
All inputs are finite; a program needn't handle non-finite values.
Results may differ from the reference program's by a relative error of at most 0.005.
Values may be sent and summed in bfloat16 or wider, within the bound.
No kernel may reach another device: no remote copies, remote signals or barrier semaphores. Data moves between devices by JAX's collectives and lax.ppermute only.
A program may use at most 256 MiB of HBM per device.

```python
import jax
import jax.numpy as jnp
from jax import lax

D = 12288
FF = 24576
TOKENS = 512


def block_scale(own_key, shape, split, smallest, largest):
    factor_of = 1.0
    for dim, parts in split:
        heights = jax.random.uniform(jax.random.fold_in(jax.random.fold_in(own_key, 6), dim), (parts,), jnp.float32, smallest / len(split), largest / len(split))
        factor_of = factor_of * jnp.repeat(jnp.exp(heights), shape[dim] // parts).reshape((-1,) + (1,) * (len(shape) - 1 - dim))
    return factor_of


def gaussian(rng, shape, spread, bound, pieces=(), held_as=jnp.bfloat16):
    array = spread * jax.random.normal(rng, shape, jnp.float32)
    if pieces:
        array = array * block_scale(rng, shape, pieces, -0.22, 0.18)
    return jnp.clip(array, -bound, bound).astype(held_as)


def setup_inputs(seed: int = 0) -> dict:
    seeds = jax.random.split(jax.random.key(seed), 6)
    return {
        "tokens": gaussian(seeds[0], (TOKENS, D), 1.0, 6.0, ((0, 16), (1, 2))),
        "out_grad": gaussian(seeds[1], (TOKENS, D), 0.5, 3.0, ((0, 16), (1, 2))),
        "w_in": gaussian(seeds[2], (D, FF), D ** -0.5, 0.0546875, ((0, 2), (1, 16))),
        "b_in": gaussian(seeds[3], (FF,), 0.5, 3.0, ((0, 16),), jnp.float32),
        "w_out": gaussian(seeds[4], (FF, D), FF ** -0.5, 0.0390625, ((0, 16), (1, 2))),
    }


tanh_scale = 0.7978845608028654
cubic_coef = 0.044715


def gelu_pair(value):
    inner = tanh_scale * (value + cubic_coef * value * value * value)
    tangent = jnp.tanh(inner)
    result = 0.5 * value * (1.0 + tangent)
    slope = 0.5 * (1.0 + tangent) + 0.5 * value * (1.0 - tangent * tangent) * tanh_scale * (1.0 + 3.0 * cubic_coef * value * value)
    return result, slope


def reference(tokens, out_grad, w_in, b_in, w_out):
    projected = jnp.dot(tokens, w_in, preferred_element_type=jnp.float32) + b_in.astype(jnp.float32)
    active_f, derivative = gelu_pair(projected)
    activated = active_f.astype(jnp.bfloat16)
    back_signal = lax.dot_general(out_grad, w_out, (((1,), (1,)), ((), ())), preferred_element_type=jnp.float32)
    proj_grad = (back_signal * derivative).astype(jnp.bfloat16)
    w_out_grad = lax.dot_general(activated, out_grad, (((0,), (0,)), ((), ())), preferred_element_type=jnp.float32).astype(jnp.bfloat16)
    w_in_grad = lax.dot_general(tokens, proj_grad, (((0,), (0,)), ((), ())), preferred_element_type=jnp.float32).astype(jnp.bfloat16)
    b_in_grad = jnp.sum(proj_grad.astype(jnp.float32), axis=0)
    in_grad = lax.dot_general(proj_grad, w_in, (((1,), (1,)), ((), ())), preferred_element_type=jnp.float32).astype(jnp.bfloat16)
    return in_grad, w_in_grad, w_out_grad, b_in_grad
```

```python
import jax
import jax.numpy as jnp
from jax import lax
from jax.sharding import PartitionSpec as P

tanh_scale = 0.7978845608028654
cubic_coef = 0.044715
ROWS = ("pipe", "tensor")
bf16, f32 = jnp.bfloat16, jnp.float32


def gelu_pair(value):
    inner = tanh_scale * (value + cubic_coef * value * value * value)
    tangent = jnp.tanh(inner)
    result = 0.5 * value * (1.0 + tangent)
    slope = 0.5 * (1.0 + tangent) + 0.5 * value * (1.0 - tangent * tangent) * tanh_scale * (
        1.0 + 3.0 * cubic_coef * value * value
    )
    return (result, slope)


def times_transpose(left, right):
    return lax.dot_general(
        left, right, (((1,), (1,)), ((), ())), preferred_element_type=f32
    )


def over_rows(left, right):
    return lax.dot_general(
        left, right, (((0,), (0,)), ((), ())), preferred_element_type=f32
    )


def shards_plain(tokens, out_grad, w_in, b_in, w_out):
    tok_all, grad_all = (
        lax.all_gather(tokens, ROWS, axis=0, tiled=True),
        lax.all_gather(out_grad, ROWS, axis=0, tiled=True),
    )
    proj_part = jnp.dot(tok_all, w_in, preferred_element_type=f32)
    signal_part = times_transpose(grad_all, w_out)
    projected = lax.psum(proj_part, "dp") + b_in
    active_f, derivative = gelu_pair(projected)
    activated = active_f.astype(bf16)
    back_signal = lax.psum(signal_part, "dp")
    proj_grad = (back_signal * derivative).astype(bf16)
    w_out_grad = over_rows(activated, grad_all).astype(bf16)
    w_in_grad = over_rows(tok_all, proj_grad).astype(bf16)
    b_in_grad = jnp.sum(proj_grad.astype(f32), axis=0)
    in_total = lax.psum_scatter(
        times_transpose(proj_grad, w_in), ROWS, scatter_dimension=0, tiled=True
    )
    return (in_total.astype(bf16), w_in_grad, w_out_grad, b_in_grad)


class Links:
    def __init__(self, pipe, tensor):
        lines = tensor // 2
        ring = []
        for y in range(lines):
            order = range(pipe) if y % 2 == 0 else range(pipe - 1, -1, -1)
            ring += [z * tensor + y * 2 for z in order]
        self.size = len(ring)
        pairs = list(zip(ring, ring[1:] + ring[:1]))
        self.fw = [(a + c, b + c) for a, b in pairs for c in range(2)]
        self.bw = [(b, a) for a, b in self.fw]
        self.core = [(t, t ^ 1) for t in range(tensor)]

    def forward(self, x):
        return lax.ppermute(x, ROWS, self.fw)

    def backward(self, x):
        return lax.ppermute(x, ROWS, self.bw)

    def sibling(self, x):
        return lax.ppermute(x, "tensor", self.core)

    def across(self, x):
        return lax.ppermute(x, "dp", [(0, 1), (1, 0)])

    def gather(self, x):
        far = self.size // 2
        half = x.shape[1] // 2
        blocks = [x]
        ahead = behind = x
        for hop in range(1, far):
            ahead, behind = self.forward(ahead), self.backward(behind)
            blocks += [ahead, behind]
        last = jnp.concatenate(
            [self.forward(ahead[:, :half]), self.backward(behind[:, half:])], axis=1
        )
        first = jnp.concatenate(blocks[: 2 * far - 3])
        rest = jnp.concatenate(blocks[2 * far - 3 :] + [last])
        return jnp.concatenate([first, rest, self.sibling(first), self.sibling(rest)])

    def scatter(self, own):
        far = self.size // 2
        rows = own.shape[0] // self.size
        half = own.shape[1] // 2
        block = lambda i: own[i * rows : (i + 1) * rows]
        opposite = block(2 * far - 1)
        down = self.backward(opposite[:, :half].astype(bf16))
        up = self.forward(opposite[:, half:].astype(bf16))
        for hop in range(far - 1, 0, -1):
            at_behind, at_ahead = block(2 * hop - 1), block(2 * hop)
            if hop == far - 1:
                pad = ((0, 0), (0, half))
                down = at_behind + jnp.pad(down.astype(f32), pad)
                up = at_ahead + jnp.pad(up.astype(f32), ((0, 0), (half, 0)))
            else:
                down, up = at_behind + down.astype(f32), at_ahead + up.astype(f32)
            down, up = self.backward(down.astype(bf16)), self.forward(up.astype(bf16))
        return block(0) + down.astype(f32) + up.astype(f32)


def shards_ring(links, parts, tokens, out_grad, w_in, b_in, w_out):
    rows = tokens.shape[0]
    step = rows // parts
    toks, grads, acts, pgs, ins = [], [], [], [], []
    for k in range(parts):
        here = slice(k * step, (k + 1) * step)
        tok = links.gather(tokens[here])
        grad = links.gather(out_grad[here])
        proj = jnp.dot(tok, w_in, preferred_element_type=f32)
        signal = times_transpose(grad, w_out)
        projected = proj + links.across(proj.astype(bf16)).astype(f32) + b_in
        active_f, derivative = gelu_pair(projected)
        back_signal = signal + links.across(signal.astype(bf16)).astype(f32)
        pg = (back_signal * derivative).astype(bf16)
        partial = times_transpose(pg, w_in)
        mine = partial.shape[0] // 2
        own = partial[:mine] + links.sibling(partial[mine:].astype(bf16)).astype(f32)
        ins.append(links.scatter(own).astype(bf16))
        toks.append(tok)
        grads.append(grad)
        acts.append(active_f.astype(bf16))
        pgs.append(pg)
    cat = jnp.concatenate
    w_out_grad = over_rows(cat(acts), cat(grads)).astype(bf16)
    w_in_grad = over_rows(cat(toks), cat(pgs)).astype(bf16)
    b_in_grad = sum(jnp.sum(pg.astype(f32), axis=0) for pg in pgs)
    return (cat(ins), w_in_grad, w_out_grad, b_in_grad)


def solution(mesh):
    in_specs = (
        P(("pipe", "tensor"), "dp"),
        P(("pipe", "tensor"), "dp"),
        P("dp", ("pipe", "tensor")),
        P(("pipe", "tensor")),
        P(("pipe", "tensor"), "dp"),
    )
    out_specs = (
        P(("pipe", "tensor"), "dp"),
        P("dp", ("pipe", "tensor")),
        P(("pipe", "tensor"), "dp"),
        P(("pipe", "tensor")),
    )
    pipe, dp, tensor = (mesh.shape[a] for a in ("pipe", "dp", "tensor"))
    if dp == 2 and tensor == 4:
        links = Links(pipe, tensor)
        body = lambda *args: shards_ring(links, 2, *args)
    else:
        body = shards_plain
    return jax.shard_map(body, mesh=mesh, in_specs=in_specs, out_specs=out_specs, check_vma=False)
```

```python
import jax
import jax.numpy as jnp
from jax import lax
from jax.experimental import pallas as pl
from jax.experimental.pallas import tpu as pltpu
from jax.sharding import PartitionSpec as P

tanh_scale = 0.7978845608028654
cubic_coef = 0.044715
ROWS = ("pipe", "tensor")
bf16, f32 = jnp.bfloat16, jnp.float32


def gelu_pair(value):
    inner = tanh_scale * (value + cubic_coef * value * value * value)
    tangent = jnp.tanh(inner)
    result = 0.5 * value * (1.0 + tangent)
    slope = 0.5 * (1.0 + tangent) + 0.5 * value * (1.0 - tangent * tangent) * tanh_scale * (
        1.0 + 3.0 * cubic_coef * value * value
    )
    return (result, slope)


def times_transpose(left, right):
    return lax.dot_general(
        left, right, (((1,), (1,)), ((), ())), preferred_element_type=f32
    )


def over_rows(left, right):
    return lax.dot_general(
        left, right, (((0,), (0,)), ((), ())), preferred_element_type=f32
    )


def shards_plain(tokens, out_grad, w_in, b_in, w_out):
    tok_all, grad_all = (
        lax.all_gather(tokens, ROWS, axis=0, tiled=True),
        lax.all_gather(out_grad, ROWS, axis=0, tiled=True),
    )
    proj_part = jnp.dot(tok_all, w_in, preferred_element_type=f32)
    signal_part = times_transpose(grad_all, w_out)
    projected = lax.psum(proj_part, "dp") + b_in
    active_f, derivative = gelu_pair(projected)
    activated = active_f.astype(bf16)
    back_signal = lax.psum(signal_part, "dp")
    proj_grad = (back_signal * derivative).astype(bf16)
    w_out_grad = over_rows(activated, grad_all).astype(bf16)
    w_in_grad = over_rows(tok_all, proj_grad).astype(bf16)
    b_in_grad = jnp.sum(proj_grad.astype(f32), axis=0)
    in_total = lax.psum_scatter(
        times_transpose(proj_grad, w_in), ROWS, scatter_dimension=0, tiled=True
    )
    return (in_total.astype(bf16), w_in_grad, w_out_grad, b_in_grad)


class Links:
    def __init__(self, pipe, tensor):
        lines = tensor // 2
        chips = []
        for y in range(lines):
            order = range(pipe) if y % 2 == 0 else range(pipe - 1, -1, -1)
            chips += [z * tensor + y * 2 for z in order]
        self.far = len(chips) // 2
        pairs = list(zip(chips, chips[1:] + chips[:1]))
        self.ring = [(a, b) for a, b in pairs] + [(b + 1, a + 1) for a, b in pairs]
        self.core = [(t, t ^ 1) for t in range(tensor)]

    def onward(self, x):
        return lax.ppermute(x, ROWS, self.ring)

    def sibling(self, x):
        return lax.ppermute(x, "tensor", self.core)

    def across(self, x):
        return lax.ppermute(x, "dp", [(0, 1), (1, 0)])


def over_rows_tiles(lefts, rights, into, first, count, tile):
    m, n = lefts[0].shape[1], rights[0].shape[1]
    parts = len(lefts)

    def kernel(*refs):
        ls, rs, o_ref = refs[:parts], refs[parts : 2 * parts], refs[-1]
        o_ref[...] = sum(over_rows(l[...], r[...]) for l, r in zip(ls, rs)).astype(bf16)

    depth = [l.shape[0] for l in lefts]
    in_specs = [pl.BlockSpec((k, tile), lambda i: (0, first + i)) for k in depth]
    in_specs += [pl.BlockSpec((k, n), lambda i: (0, 0)) for k in depth]
    args = list(lefts) + list(rights)
    alias = {}
    if into is not None:
        alias = {len(args): 0}
        args.append(into)
        in_specs.append(pl.BlockSpec(memory_space=pl.ANY))
    return pl.pallas_call(
        kernel,
        grid=(count,),
        in_specs=in_specs,
        out_specs=pl.BlockSpec((tile, n), lambda i: (first + i, 0)),
        out_shape=jax.ShapeDtypeStruct((m, n), bf16),
        input_output_aliases=alias,
        compiler_params=pltpu.CompilerParams(vmem_limit_bytes=40 << 20),
        cost_estimate=pl.CostEstimate(
            flops=2 * sum(depth) * count * tile * n,
            bytes_accessed=2 * (sum(depth) * (count * tile + n) + count * tile * n),
            transcendentals=0,
        ),
    )(*args)


def after(x, *others):
    return lax.optimization_barrier((x, others))[0]


def shards_ring(links, tokens, out_grad, w_in, b_in, w_out):
    far = links.far
    step = tokens.shape[0] // 2
    cat = jnp.concatenate

    def together(send, blocks):
        sizes = [b.shape[0] for b in blocks]
        got = send(cat(blocks))
        return [got[sum(sizes[:i]) : sum(sizes[: i + 1])] for i in range(len(sizes))]

    def apart(send, blocks):
        return [send(b) for b in blocks]

    def gather(chips, move, waits):
        got = {0: chips}
        for d in range(1, far + 1):
            out = got[d - 1]
            if d == far:
                out = [b[:step] for b in out]
            wait = waits(d, got)
            if wait is not None:
                out = after(out, wait)
            got[d] = move(links.onward, out)
        rows = []
        for i in range(len(chips)):
            early = cat([got[d][i] for d in range(1, far - 1)])
            late = cat([got[d][i] for d in range(far - 1, far + 1)])
            mine, theirs = chips[i][:step], chips[i][step:]
            others = [links.sibling(early), links.sibling(late)]
            rows.append(cat([mine, *others, theirs, early, late]))
        return rows, got

    def other_half(own):
        return links.across(own.astype(bf16))

    def project(rows):
        return jnp.dot(rows, w_in, preferred_element_type=f32)

    def signals(rows):
        return times_transpose(rows, w_out)

    def activate(p, p_other):
        return gelu_pair(p + p_other.astype(f32) + b_in)

    def backprop(s, s_other, derivative):
        pg = ((s + s_other.astype(f32)) * derivative).astype(bf16)
        return pg, jnp.sum(pg.astype(f32), axis=0)

    tok_sib, grad_sib = links.sibling(tokens), links.sibling(out_grad)
    chunk = lambda x, y, k: cat([x[k * step : (k + 1) * step], y[k * step : (k + 1) * step]])
    chips = [[chunk(tokens, tok_sib, k), chunk(out_grad, grad_sib, k)] for k in range(2)]

    (tok1, grad1), got1 = gather(chips[0], apart, lambda *_: None)
    done = {}

    def waits(d, got):
        if d == 1:
            return got1[far - 1]
        if d == 2:
            done["p"] = project(tok1)
            return done["p"]
        if d == 3:
            done["s"] = signals(after(grad1, got[1], done["p"]))
            done["px"] = other_half(after(done["p"], got[1]))
            return done["s"]
        return done["px"]

    (tok2, grad2), got2 = gather(chips[1], together, waits)
    s1x = after(other_half(done["s"]), got2[far])
    p2 = project(tok2)
    act1, slope1 = activate(done["p"], done["px"])
    pg1, sum1 = backprop(done["s"], s1x, slope1)
    act1, pg1, sum1 = lax.optimization_barrier((act1.astype(bf16), pg1, sum1))
    s2 = signals(after(grad2, pg1, p2))
    parts = lambda x: [x[: 8 * step], x[8 * step :]]
    p2x, s2x = [[other_half(h) for h in parts(x)] for x in (p2, s2)]

    def own_sums(pg, beside=None):
        partial = times_transpose(pg, w_in)
        if beside is not None:
            partial, beside = lax.optimization_barrier((partial, beside))
        theirs = links.sibling(partial.astype(bf16)[8 * step :])
        return partial, partial[: 8 * step] + theirs.astype(f32), beside

    def scatter(own, beside):
        running = own[(2 * far - 1) * step :].astype(bf16)
        for n, d in enumerate(range(far - 1, -1, -1)):
            work = beside(n, running)
            running = links.onward(running)
            if d == 0:
                ours = own[:step] + running[step:].astype(f32)
                return (ours + links.sibling(running[:step]).astype(f32)).astype(bf16), work
            here = own[(2 * d - 1) * step : (2 * d + 1) * step]
            if n == 0:
                first = here[:step] + running.astype(f32)
                running = cat([first.astype(bf16), here[step:].astype(bf16)])
            else:
                running = (here + running.astype(f32)).astype(bf16)
            if work is not None:
                running = after(running, work)

    part1, own1, p2x[1] = own_sums(after(pg1, s2, p2x[0]), p2x[1])
    act2, slope2 = activate(p2, cat(p2x))
    act2, slope2 = lax.optimization_barrier((act2.astype(bf16), slope2))
    made = {}

    def beside1(n, ready):
        if n == 3:
            pg2, made["sum2"] = backprop(s2, cat(after(s2x, ready, made["out"])), slope2)
            made["pg2"] = pg2
            made["part2"], made["own2"], _ = own_sums(pg2)
            return made["part2"]
        wait = made.get("part2", made.get("out", part1))
        a1, a2 = after((act1, act2), ready, wait)
        index = n
        made["out"] = over_rows_tiles(
            [a1, a2], [grad1, grad2], made.get("out"), 2 * index, 2, act1.shape[1] // 6
        )
        pairing = {0: 0, 3 - 1: 1}.get(n)
        if pairing is not None:
            made["out"], s2x[pairing] = lax.optimization_barrier((made["out"], s2x[pairing]))
        return made["out"]

    in1, _ = scatter(own1, beside1)

    def beside2(n, ready):
        if n == 3:
            return None
        t1, t2 = after((tok1, tok2), ready, made.get("in", made["out"]))
        made["in"] = over_rows_tiles(
            [t1, t2], [pg1, made["pg2"]], made.get("in"), 2 * n, 2, tokens.shape[1] // 6
        )
        return made["in"]

    in2, _ = scatter(made["own2"], beside2)
    return (cat([in1, in2]), made["in"], made["out"], sum1 + made["sum2"])


def solution(mesh):
    in_specs = (
        P(("pipe", "tensor"), "dp"),
        P(("pipe", "tensor"), "dp"),
        P("dp", ("pipe", "tensor")),
        P(("pipe", "tensor")),
        P(("pipe", "tensor"), "dp"),
    )
    out_specs = (
        P(("pipe", "tensor"), "dp"),
        P("dp", ("pipe", "tensor")),
        P(("pipe", "tensor"), "dp"),
        P(("pipe", "tensor")),
    )
    pipe, dp, tensor = (mesh.shape[a] for a in ("pipe", "dp", "tensor"))
    if dp == 2 and tensor == 4:
        links = Links(pipe, tensor)
        body = lambda *args: shards_ring(links, *args)
    else:
        body = shards_plain
    return jax.shard_map(body, mesh=mesh, in_specs=in_specs, out_specs=out_specs, check_vma=False)
```

```python
import jax
import jax.numpy as jnp
from jax import lax
from jax.experimental import pallas as pl
from jax.experimental.pallas import tpu as pltpu
from jax.sharding import PartitionSpec as P

tanh_scale = 0.7978845608028654
cubic_coef = 0.044715
ROWS = ("pipe", "tensor")
bf16, f32 = jnp.bfloat16, jnp.float32


def gelu_pair(value):
    inner = tanh_scale * (value + cubic_coef * value * value * value)
    tangent = jnp.tanh(inner)
    result = 0.5 * value * (1.0 + tangent)
    slope = 0.5 * (1.0 + tangent) + 0.5 * value * (1.0 - tangent * tangent) * tanh_scale * (
        1.0 + 3.0 * cubic_coef * value * value
    )
    return (result, slope)


def times_transpose(left, right):
    return lax.dot_general(
        left, right, (((1,), (1,)), ((), ())), preferred_element_type=f32
    )


def over_rows(left, right):
    return lax.dot_general(
        left, right, (((0,), (0,)), ((), ())), preferred_element_type=f32
    )


def shards_plain(tokens, out_grad, w_in, b_in, w_out):
    tok_all, grad_all = (
        lax.all_gather(tokens, ROWS, axis=0, tiled=True),
        lax.all_gather(out_grad, ROWS, axis=0, tiled=True),
    )
    proj_part = jnp.dot(tok_all, w_in, preferred_element_type=f32)
    signal_part = times_transpose(grad_all, w_out)
    projected = lax.psum(proj_part, "dp") + b_in
    active_f, derivative = gelu_pair(projected)
    activated = active_f.astype(bf16)
    back_signal = lax.psum(signal_part, "dp")
    proj_grad = (back_signal * derivative).astype(bf16)
    w_out_grad = over_rows(activated, grad_all).astype(bf16)
    w_in_grad = over_rows(tok_all, proj_grad).astype(bf16)
    b_in_grad = jnp.sum(proj_grad.astype(f32), axis=0)
    in_total = lax.psum_scatter(
        times_transpose(proj_grad, w_in), ROWS, scatter_dimension=0, tiled=True
    )
    return (in_total.astype(bf16), w_in_grad, w_out_grad, b_in_grad)


class Links:
    def __init__(self, pipe, tensor):
        lines = tensor // 2
        chips = []
        for y in range(lines):
            order = range(pipe) if y % 2 == 0 else range(pipe - 1, -1, -1)
            chips += [z * tensor + y * 2 for z in order]
        self.far = len(chips) // 2
        pairs = list(zip(chips, chips[1:] + chips[:1]))
        self.ring = [(a, b) for a, b in pairs] + [(b + 1, a + 1) for a, b in pairs]
        self.core = [(t, t ^ 1) for t in range(tensor)]

    def onward(self, x):
        return lax.ppermute(x, ROWS, self.ring)

    def sibling(self, x):
        return lax.ppermute(x, "tensor", self.core)

    def across(self, x):
        return lax.ppermute(x, "dp", [(0, 1), (1, 0)])


def over_rows_tiles(lefts, rights, into, first, count, tile):
    m, n = lefts[0].shape[1], rights[0].shape[1]
    parts = len(lefts)

    def kernel(*refs):
        ls, rs, o_ref = refs[:parts], refs[parts : 2 * parts], refs[-1]
        o_ref[...] = sum(over_rows(l[...], r[...]) for l, r in zip(ls, rs)).astype(bf16)

    depth = [l.shape[0] for l in lefts]
    in_specs = [pl.BlockSpec((k, tile), lambda i: (0, first + i)) for k in depth]
    in_specs += [pl.BlockSpec((k, n), lambda i: (0, 0)) for k in depth]
    args = list(lefts) + list(rights)
    alias = {}
    if into is not None:
        alias = {len(args): 0}
        args.append(into)
        in_specs.append(pl.BlockSpec(memory_space=pl.ANY))
    return pl.pallas_call(
        kernel,
        grid=(count,),
        in_specs=in_specs,
        out_specs=pl.BlockSpec((tile, n), lambda i: (first + i, 0)),
        out_shape=jax.ShapeDtypeStruct((m, n), bf16),
        input_output_aliases=alias,
        compiler_params=pltpu.CompilerParams(vmem_limit_bytes=40 << 20),
        cost_estimate=pl.CostEstimate(
            flops=2 * sum(depth) * count * tile * n,
            bytes_accessed=2 * (sum(depth) * (count * tile + n) + count * tile * n),
            transcendentals=0,
        ),
    )(*args)


def after(x, *others):
    return lax.optimization_barrier((x, others))[0]


def back_rows(pg, w_in, tile):
    rows, hidden = pg.shape
    width = w_in.shape[0]
    half = rows // 2

    def kernel(pg_ref, w_ref, keep_ref, send_ref):
        out = times_transpose(pg_ref[...], w_ref[...])
        keep_ref[...] = out[:half]
        send_ref[...] = out[half:].astype(bf16)

    return pl.pallas_call(
        kernel,
        grid=(width // tile,),
        in_specs=[
            pl.BlockSpec((rows, hidden), lambda i: (0, 0)),
            pl.BlockSpec((tile, hidden), lambda i: (i, 0)),
        ],
        out_specs=[pl.BlockSpec((half, tile), lambda i: (0, i))] * 2,
        out_shape=[
            jax.ShapeDtypeStruct((half, width), f32),
            jax.ShapeDtypeStruct((half, width), bf16),
        ],
        compiler_params=pltpu.CompilerParams(vmem_limit_bytes=40 << 20),
        cost_estimate=pl.CostEstimate(
            flops=2 * rows * hidden * width,
            bytes_accessed=2 * hidden * (rows + width) + 6 * half * width,
            transcendentals=0,
        ),
    )(pg, w_in)


def shards_ring(links, tokens, out_grad, w_in, b_in, w_out):
    far = links.far
    step = tokens.shape[0] // 2
    cat, pair = jnp.concatenate, lambda *xs: lax.optimization_barrier(xs)

    def together(send, blocks):
        sizes = [b.shape[0] for b in blocks]
        got = send(cat(blocks))
        return [got[sum(sizes[:i]) : sum(sizes[: i + 1])] for i in range(len(sizes))]

    def apart(send, blocks):
        return [send(b) for b in blocks]

    def gather(chips, move, waits):
        got = {0: chips}
        for d in range(1, far + 1):
            out = got[d - 1]
            if d == far:
                out = [b[:step] for b in out]
            wait = waits(d, got)
            if wait is not None:
                out = after(out, wait)
            got[d] = move(links.onward, out)
        rows = []
        for i in range(len(chips)):
            early = cat([got[d][i] for d in range(1, far - 1)])
            late = cat([got[d][i] for d in range(far - 1, far + 1)])
            mine, theirs = chips[i][:step], chips[i][step:]
            others = [links.sibling(early), links.sibling(late)]
            rows.append(cat([mine, *others, theirs, early, late]))
        return rows, got

    def other_half(own):
        return links.across(own.astype(bf16))

    def project(rows):
        return jnp.dot(rows, w_in, preferred_element_type=f32)

    def signals(rows):
        return times_transpose(rows, w_out)

    def activate(p, p_other):
        return gelu_pair(p + p_other.astype(f32) + b_in)

    def backprop(s, s_other, derivative):
        pg = ((s + s_other.astype(f32)) * derivative).astype(bf16)
        return pg, jnp.sum(pg.astype(f32), axis=0)

    tok_sib, grad_sib = links.sibling(tokens), links.sibling(out_grad)
    chunk = lambda x, y, k: cat([x[k * step : (k + 1) * step], y[k * step : (k + 1) * step]])
    chips = [[chunk(tokens, tok_sib, k), chunk(out_grad, grad_sib, k)] for k in range(2)]

    (tok1, grad1), got1 = gather(chips[0], apart, lambda *_: None)
    done = {}

    def waits(d, got):
        if d == 1:
            return got1[far - 1]
        if d == 2:
            done["p"] = project(tok1)
            return done["p"]
        if d == 3:
            done["s"] = signals(after(grad1, got[1], done["p"]))
            done["px"] = other_half(after(done["p"], got[1]))
            return done["s"]
        return done["px"]

    (tok2, grad2), got2 = gather(chips[1], together, waits)
    s1x = after(other_half(done["s"]), got2[far])
    p2 = project(tok2)
    act1, slope1 = activate(done["p"], done["px"])
    pg1, sum1 = backprop(done["s"], s1x, slope1)
    act1, pg1, sum1 = lax.optimization_barrier((act1.astype(bf16), pg1, sum1))
    s2 = signals(after(grad2, pg1, p2))
    def own_sums(pg, *beside):
        keep, send, *beside = pair(*back_rows(pg, w_in, w_in.shape[0] // 6), *beside)
        return send, keep + links.sibling(send).astype(f32), beside

    def scatter(own, beside):
        running = own[(2 * far - 1) * step :].astype(bf16)
        for n, d in enumerate(range(far - 1, -1, -1)):
            work = beside(n, running)
            running = links.onward(running)
            if d == 0:
                ours = own[:step] + running[step:].astype(f32)
                return (ours + links.sibling(running[:step]).astype(f32)).astype(bf16), work
            here = own[(2 * d - 1) * step : (2 * d + 1) * step]
            if n == 0:
                first = here[:step] + running.astype(f32)
                running = cat([first.astype(bf16), here[step:].astype(bf16)])
            else:
                running = (here + running.astype(f32)).astype(bf16)
            if work is not None:
                running = after(running, work)

    def pieces(x, n):
        size = x.shape[0] // n
        return [x[i * size : (i + 1) * size] for i in range(n)]

    p2_a, p2_b = pieces(p2, 2)
    s2, p2x_a = pair(s2, other_half(p2_a))
    s2_first, *s2_rest = pieces(s2, 4)
    part1, own1, (p2x_b, *s2x) = own_sums(
        after(pg1, s2), other_half(after(p2_b, s2)), other_half(s2_first)
    )
    act2, slope2 = activate(p2, cat([p2x_a, p2x_b]))
    act2, slope2 = pair(act2.astype(bf16), slope2)
    made = {}

    def beside1(n, ready):
        if n == 3:
            pg2, made["sum2"] = backprop(s2, cat(after(s2x, ready)), slope2)
            made["pg2"] = pg2
            made["part2"], made["own2"], _ = own_sums(pg2)
            return made["part2"]
        wait = made.get("out", part1)
        a1, a2 = after((act1, act2), ready, wait)
        out = over_rows_tiles(
            [a1, a2], [grad1, grad2], made.get("out"), 2 * n, 2, act1.shape[1] // 6
        )
        made["out"], more = pair(out, other_half(after(s2_rest[n], wait)))
        s2x.append(more)
        return made["out"]

    in1, _ = scatter(own1, beside1)

    def beside2(n, ready):
        if n == 3:
            return None
        t1, t2 = after((tok1, tok2), ready, made.get("in", made["out"]))
        made["in"] = over_rows_tiles(
            [t1, t2], [pg1, made["pg2"]], made.get("in"), 2 * n, 2, tokens.shape[1] // 6
        )
        return made["in"]

    in2, _ = scatter(made["own2"], beside2)
    return (cat([in1, in2]), made["in"], made["out"], sum1 + made["sum2"])


def solution(mesh):
    in_specs = (
        P(("pipe", "tensor"), "dp"),
        P(("pipe", "tensor"), "dp"),
        P("dp", ("pipe", "tensor")),
        P(("pipe", "tensor")),
        P(("pipe", "tensor"), "dp"),
    )
    out_specs = (
        P(("pipe", "tensor"), "dp"),
        P("dp", ("pipe", "tensor")),
        P(("pipe", "tensor"), "dp"),
        P(("pipe", "tensor")),
    )
    pipe, dp, tensor = (mesh.shape[a] for a in ("pipe", "dp", "tensor"))
    if dp == 2 and tensor == 4:
        links = Links(pipe, tensor)
        body = lambda *args: shards_ring(links, *args)
    else:
        body = shards_plain
    return jax.shard_map(body, mesh=mesh, in_specs=in_specs, out_specs=out_specs, check_vma=False)
```

```python
import jax
import jax.numpy as jnp
from jax import lax
from jax.experimental import pallas as pl
from jax.experimental.pallas import tpu as pltpu
from jax.sharding import PartitionSpec as P

tanh_scale = 0.7978845608028654
cubic_coef = 0.044715
ROWS = ("pipe", "tensor")
bf16, f32 = jnp.bfloat16, jnp.float32


def gelu_pair(value):
    inner = tanh_scale * (value + cubic_coef * value * value * value)
    tangent = jnp.tanh(inner)
    result = 0.5 * value * (1.0 + tangent)
    slope = 0.5 * (1.0 + tangent) + 0.5 * value * (1.0 - tangent * tangent) * tanh_scale * (
        1.0 + 3.0 * cubic_coef * value * value
    )
    return (result, slope)


def times_transpose(left, right):
    return lax.dot_general(
        left, right, (((1,), (1,)), ((), ())), preferred_element_type=f32
    )


def over_rows(left, right):
    return lax.dot_general(
        left, right, (((0,), (0,)), ((), ())), preferred_element_type=f32
    )


def shards_plain(tokens, out_grad, w_in, b_in, w_out):
    tok_all, grad_all = (
        lax.all_gather(tokens, ROWS, axis=0, tiled=True),
        lax.all_gather(out_grad, ROWS, axis=0, tiled=True),
    )
    proj_part = jnp.dot(tok_all, w_in, preferred_element_type=f32)
    signal_part = times_transpose(grad_all, w_out)
    projected = lax.psum(proj_part, "dp") + b_in
    active_f, derivative = gelu_pair(projected)
    activated = active_f.astype(bf16)
    back_signal = lax.psum(signal_part, "dp")
    proj_grad = (back_signal * derivative).astype(bf16)
    w_out_grad = over_rows(activated, grad_all).astype(bf16)
    w_in_grad = over_rows(tok_all, proj_grad).astype(bf16)
    b_in_grad = jnp.sum(proj_grad.astype(f32), axis=0)
    in_total = lax.psum_scatter(
        times_transpose(proj_grad, w_in), ROWS, scatter_dimension=0, tiled=True
    )
    return (in_total.astype(bf16), w_in_grad, w_out_grad, b_in_grad)


class Links:
    def __init__(self, pipe, tensor):
        lines = tensor // 2
        chips = []
        for y in range(lines):
            order = range(pipe) if y % 2 == 0 else range(pipe - 1, -1, -1)
            chips += [z * tensor + y * 2 for z in order]
        self.far = len(chips) // 2
        pairs = list(zip(chips, chips[1:] + chips[:1]))
        self.ring = [(a, b) for a, b in pairs] + [(b + 1, a + 1) for a, b in pairs]
        self.core = [(t, t ^ 1) for t in range(tensor)]

    def onward(self, x):
        return lax.ppermute(x, ROWS, self.ring)

    def sibling(self, x):
        return lax.ppermute(x, "tensor", self.core)

    def across(self, x):
        return lax.ppermute(x, "dp", [(0, 1), (1, 0)])


def over_rows_tiles(lefts, rights, into, first, count, tile):
    m, n = lefts[0].shape[1], rights[0].shape[1]
    parts = len(lefts)

    def kernel(*refs):
        ls, rs, o_ref = refs[:parts], refs[parts : 2 * parts], refs[-1]
        o_ref[...] = sum(over_rows(l[...], r[...]) for l, r in zip(ls, rs)).astype(bf16)

    depth = [l.shape[0] for l in lefts]
    in_specs = [pl.BlockSpec((k, tile), lambda i: (0, first + i)) for k in depth]
    in_specs += [pl.BlockSpec((k, n), lambda i: (0, 0)) for k in depth]
    args = list(lefts) + list(rights)
    alias = {}
    if into is not None:
        alias = {len(args): 0}
        args.append(into)
        in_specs.append(pl.BlockSpec(memory_space=pl.ANY))
    return pl.pallas_call(
        kernel,
        grid=(count,),
        in_specs=in_specs,
        out_specs=pl.BlockSpec((tile, n), lambda i: (first + i, 0)),
        out_shape=jax.ShapeDtypeStruct((m, n), bf16),
        input_output_aliases=alias,
        compiler_params=pltpu.CompilerParams(vmem_limit_bytes=40 << 20),
        cost_estimate=pl.CostEstimate(
            flops=2 * sum(depth) * count * tile * n,
            bytes_accessed=2 * (sum(depth) * (count * tile + n) + count * tile * n),
            transcendentals=0,
        ),
    )(*args)


def after(x, *others):
    return lax.optimization_barrier((x, others))[0]


def back_rows(pg, w_in, tile):
    rows, hidden = pg.shape
    width = w_in.shape[0]
    half = rows // 2

    def kernel(pg_ref, w_ref, keep_ref, send_ref):
        out = times_transpose(pg_ref[...], w_ref[...])
        keep_ref[...] = out[:half]
        send_ref[...] = out[half:].astype(bf16)

    return pl.pallas_call(
        kernel,
        grid=(width // tile,),
        in_specs=[
            pl.BlockSpec((rows, hidden), lambda i: (0, 0)),
            pl.BlockSpec((tile, hidden), lambda i: (i, 0)),
        ],
        out_specs=[pl.BlockSpec((half, tile), lambda i: (0, i))] * 2,
        out_shape=[
            jax.ShapeDtypeStruct((half, width), f32),
            jax.ShapeDtypeStruct((half, width), bf16),
        ],
        compiler_params=pltpu.CompilerParams(vmem_limit_bytes=40 << 20),
        cost_estimate=pl.CostEstimate(
            flops=2 * rows * hidden * width,
            bytes_accessed=2 * hidden * (rows + width) + 6 * half * width,
            transcendentals=0,
        ),
    )(pg, w_in)


def shards_ring(links, tokens, out_grad, w_in, b_in, w_out):
    far = links.far
    step = tokens.shape[0] // 2
    cat, pair = jnp.concatenate, lambda *xs: lax.optimization_barrier(xs)

    def onward(block, d, *others):
        if d == far:
            block = block[:step]
        return links.onward(after(block, *others) if others else block)

    def rows_of(got):
        early, late = cat(got[1 : far - 1]), cat(got[far - 1 :])
        others = [links.sibling(early), links.sibling(late)]
        return cat([got[0][:step], *others, got[0][step:], early, late])

    def other_half(own):
        return links.across(own.astype(bf16))

    def project(rows, cols=slice(None)):
        return jnp.dot(rows, w_in[:, cols], preferred_element_type=f32)

    def signals(rows, cols=slice(None)):
        return times_transpose(rows, w_out[cols])

    def activate(p, p_other, cols=slice(None)):
        return gelu_pair(p + p_other.astype(f32) + b_in[cols])

    def backprop(s, s_other, derivative):
        pg = ((s + s_other.astype(f32)) * derivative).astype(bf16)
        return pg, jnp.sum(pg.astype(f32), axis=0)

    tok_sib, grad_sib = links.sibling(tokens), links.sibling(out_grad)
    chunk = lambda x, y, k: cat([x[k * step : (k + 1) * step], y[k * step : (k + 1) * step]])
    toks, grads = [
        [[chunk(x, y, k)] for k in range(2)] for x, y in ((tokens, tok_sib), (out_grad, grad_sib))
    ]

    for d in range(1, far + 1):
        toks[0].append(onward(toks[0][-1], d))
        grads[0].append(onward(grads[0][-1], d))
    tok1, grad1 = rows_of(toks[0]), rows_of(grads[0])

    t, g = toks[1], grads[1]
    halves = [slice(0, w_in.shape[1] // 2), slice(w_in.shape[1] // 2, None)]
    t.append(onward(t[0], 1, toks[0][far - 1]))
    g.append(onward(g[0], 1, grads[0][far - 1]))
    p1, t[1], g[1] = pair(project(tok1), t[1], g[1])
    t.append(onward(t[1], 2))
    g.append(onward(g[1], 2))
    for d in range(3, far):
        t.append(onward(t[-1], d))
    p1x = other_half(p1)
    s_a, g[2], t[far - 1] = pair(signals(after(grad1, t[2], p1), halves[0]), g[2], t[far - 1])
    for d in range(3, far):
        g.append(onward(g[-1], d))
    t.append(onward(t[-1], far))
    s_b, g[far - 1], t[far] = pair(signals(after(grad1, s_a), halves[1]), g[far - 1], t[far])
    s_ax, s_bx = other_half(s_a), other_half(s_b)
    g.append(onward(g[-1], far))
    tok2, grad2 = rows_of(t), rows_of(g)
    p2, s_ax = pair(project(tok2), s_ax)
    s2 = signals(after(grad2, p2))
    act1, slope1 = activate(p1, p1x)
    pg1, sum1 = backprop(cat([s_a, s_b], axis=1), cat([s_ax, s_bx], axis=1), slope1)
    act1, pg1, sum1 = pair(act1.astype(bf16), pg1, sum1)

    def own_sums(pg, *beside):
        keep, send, *beside = pair(*back_rows(pg, w_in, w_in.shape[0] // 6), *beside)
        return send, keep + links.sibling(send).astype(f32), beside

    def scatter(own, beside):
        running = own[(2 * far - 1) * step :].astype(bf16)
        for n, d in enumerate(range(far - 1, -1, -1)):
            work = beside(n, running)
            running = links.onward(running)
            if d == 0:
                ours = own[:step] + running[step:].astype(f32)
                return (ours + links.sibling(running[:step]).astype(f32)).astype(bf16), work
            here = own[(2 * d - 1) * step : (2 * d + 1) * step]
            if n == 0:
                first = here[:step] + running.astype(f32)
                running = cat([first.astype(bf16), here[step:].astype(bf16)])
            else:
                running = (here + running.astype(f32)).astype(bf16)
            if work is not None:
                running = after(running, work)

    def pieces(x, n):
        size = x.shape[0] // n
        return [x[i * size : (i + 1) * size] for i in range(n)]

    p2_a, p2_b = pieces(p2, 2)
    s2, p2x_a = pair(s2, other_half(p2_a))
    cuts = (0, 4 * step, 10 * step, 16 * step)
    s2_first, *s2_rest = [s2[a:b] for a, b in zip(cuts, cuts[1:])]
    part1, own1, (p2x_b, *s2x) = own_sums(
        after(pg1, s2), other_half(after(p2_b, s2)), other_half(s2_first)
    )
    act2, slope2 = activate(p2, cat([p2x_a, p2x_b]))
    act2, slope2 = pair(act2.astype(bf16), slope2)
    made = {}

    def beside1(n, ready):
        if n == 2:
            pg2, made["sum2"] = backprop(s2, cat(after(s2x, ready)), slope2)
            made["pg2"] = pg2
            made["keep"], made["send"] = pair(*back_rows(pg2, w_in, w_in.shape[0] // 6))
            made["theirs"] = links.sibling(made["send"])
            return made["send"]
        wait = made.get("send", made.get("out", part1))
        a1, a2 = after((act1, act2), ready, wait)
        out = over_rows_tiles(
            [a1, a2], [grad1, grad2], made.get("out"), 2 * min(n, 2), 2, act1.shape[1] // 6
        )
        if n == 3:
            made["out"], made["theirs"] = pair(out, made["theirs"])
        else:
            made["out"], more = pair(out, other_half(after(s2_rest[n], wait)))
            s2x.append(more)
        return made["out"]

    in1, _ = scatter(own1, beside1)
    own2 = made["keep"] + made["theirs"].astype(f32)

    def beside2(n, ready):
        if n == 3:
            return None
        t1, t2 = after((tok1, tok2), ready, made.get("in", made["out"]))
        made["in"] = over_rows_tiles(
            [t1, t2], [pg1, made["pg2"]], made.get("in"), 2 * n, 2, tokens.shape[1] // 6
        )
        return made["in"]

    in2, _ = scatter(own2, beside2)
    return (cat([in1, in2]), made["in"], made["out"], sum1 + made["sum2"])


def solution(mesh):
    in_specs = (
        P(("pipe", "tensor"), "dp"),
        P(("pipe", "tensor"), "dp"),
        P("dp", ("pipe", "tensor")),
        P(("pipe", "tensor")),
        P(("pipe", "tensor"), "dp"),
    )
    out_specs = (
        P(("pipe", "tensor"), "dp"),
        P("dp", ("pipe", "tensor")),
        P(("pipe", "tensor"), "dp"),
        P(("pipe", "tensor")),
    )
    pipe, dp, tensor = (mesh.shape[a] for a in ("pipe", "dp", "tensor"))
    if dp == 2 and tensor == 4:
        links = Links(pipe, tensor)
        body = lambda *args: shards_ring(links, *args)
    else:
        body = shards_plain
    return jax.shard_map(body, mesh=mesh, in_specs=in_specs, out_specs=out_specs, check_vma=False)
```

```python
import jax
import jax.numpy as jnp
from jax import lax
from jax.experimental import pallas as pl
from jax.experimental.pallas import tpu as pltpu
from jax.sharding import PartitionSpec as P

tanh_scale = 0.7978845608028654
cubic_coef = 0.044715
ROWS = ("pipe", "tensor")
bf16, f32 = jnp.bfloat16, jnp.float32


def gelu_pair(value):
    inner = tanh_scale * (value + cubic_coef * value * value * value)
    tangent = jnp.tanh(inner)
    result = 0.5 * value * (1.0 + tangent)
    slope = 0.5 * (1.0 + tangent) + 0.5 * value * (1.0 - tangent * tangent) * tanh_scale * (
        1.0 + 3.0 * cubic_coef * value * value
    )
    return (result, slope)


def times_transpose(left, right):
    return lax.dot_general(
        left, right, (((1,), (1,)), ((), ())), preferred_element_type=f32
    )


def over_rows(left, right):
    return lax.dot_general(
        left, right, (((0,), (0,)), ((), ())), preferred_element_type=f32
    )


def shards_plain(tokens, out_grad, w_in, b_in, w_out):
    tok_all, grad_all = (
        lax.all_gather(tokens, ROWS, axis=0, tiled=True),
        lax.all_gather(out_grad, ROWS, axis=0, tiled=True),
    )
    proj_part = jnp.dot(tok_all, w_in, preferred_element_type=f32)
    signal_part = times_transpose(grad_all, w_out)
    projected = lax.psum(proj_part, "dp") + b_in
    active_f, derivative = gelu_pair(projected)
    activated = active_f.astype(bf16)
    back_signal = lax.psum(signal_part, "dp")
    proj_grad = (back_signal * derivative).astype(bf16)
    w_out_grad = over_rows(activated, grad_all).astype(bf16)
    w_in_grad = over_rows(tok_all, proj_grad).astype(bf16)
    b_in_grad = jnp.sum(proj_grad.astype(f32), axis=0)
    in_total = lax.psum_scatter(
        times_transpose(proj_grad, w_in), ROWS, scatter_dimension=0, tiled=True
    )
    return (in_total.astype(bf16), w_in_grad, w_out_grad, b_in_grad)


class Links:
    def __init__(self, pipe, tensor):
        lines = tensor // 2
        chips = []
        for y in range(lines):
            order = range(pipe) if y % 2 == 0 else range(pipe - 1, -1, -1)
            chips += [z * tensor + y * 2 for z in order]
        self.far = len(chips) // 2
        pairs = list(zip(chips, chips[1:] + chips[:1]))
        self.ring = [(a, b) for a, b in pairs] + [(b + 1, a + 1) for a, b in pairs]
        self.core = [(t, t ^ 1) for t in range(tensor)]

    def onward(self, x):
        return lax.ppermute(x, ROWS, self.ring)

    def sibling(self, x):
        return lax.ppermute(x, "tensor", self.core)

    def across(self, x):
        return lax.ppermute(x, "dp", [(0, 1), (1, 0)])


def over_rows_tiles(lefts, rights, into, first, count, tile):
    m, n = lefts[0].shape[1], rights[0].shape[1]
    parts = len(lefts)

    def kernel(*refs):
        ls, rs, o_ref = refs[:parts], refs[parts : 2 * parts], refs[-1]
        o_ref[...] = sum(over_rows(l[...], r[...]) for l, r in zip(ls, rs)).astype(bf16)

    depth = [l.shape[0] for l in lefts]
    in_specs = [pl.BlockSpec((k, tile), lambda i: (0, first + i)) for k in depth]
    in_specs += [pl.BlockSpec((k, n), lambda i: (0, 0)) for k in depth]
    args = list(lefts) + list(rights)
    alias = {}
    if into is not None:
        alias = {len(args): 0}
        args.append(into)
        in_specs.append(pl.BlockSpec(memory_space=pl.ANY))
    return pl.pallas_call(
        kernel,
        grid=(count,),
        in_specs=in_specs,
        out_specs=pl.BlockSpec((tile, n), lambda i: (first + i, 0)),
        out_shape=jax.ShapeDtypeStruct((m, n), bf16),
        input_output_aliases=alias,
        compiler_params=pltpu.CompilerParams(vmem_limit_bytes=40 << 20),
        cost_estimate=pl.CostEstimate(
            flops=2 * sum(depth) * count * tile * n,
            bytes_accessed=2 * (sum(depth) * (count * tile + n) + count * tile * n),
            transcendentals=0,
        ),
    )(*args)


def after(x, *others):
    return lax.optimization_barrier((x, others))[0]


def back_rows(pg, w_in, tile):
    rows, hidden = pg.shape
    width = w_in.shape[0]
    half = rows // 2

    def kernel(pg_ref, w_ref, keep_ref, send_ref):
        out = times_transpose(pg_ref[...], w_ref[...])
        keep_ref[...] = out[:half]
        send_ref[...] = out[half:].astype(bf16)

    return pl.pallas_call(
        kernel,
        grid=(width // tile,),
        in_specs=[
            pl.BlockSpec((rows, hidden), lambda i: (0, 0)),
            pl.BlockSpec((tile, hidden), lambda i: (i, 0)),
        ],
        out_specs=[pl.BlockSpec((half, tile), lambda i: (0, i))] * 2,
        out_shape=[
            jax.ShapeDtypeStruct((half, width), f32),
            jax.ShapeDtypeStruct((half, width), bf16),
        ],
        compiler_params=pltpu.CompilerParams(vmem_limit_bytes=40 << 20),
        cost_estimate=pl.CostEstimate(
            flops=2 * rows * hidden * width,
            bytes_accessed=2 * hidden * (rows + width) + 6 * half * width,
            transcendentals=0,
        ),
    )(pg, w_in)


def shards_ring(links, tokens, out_grad, w_in, b_in, w_out):
    far = links.far
    step = tokens.shape[0] // 2
    cat, pair = jnp.concatenate, lambda *xs: lax.optimization_barrier(xs)

    def onward(block, d, *others):
        if d == far:
            block = block[:step]
        return links.onward(after(block, *others) if others else block)

    def rows_of(got, last_apart=False):
        early, late = cat(got[1 : far - 1]), cat(got[far - 1 :])
        ends = got[far - 1 :] if last_apart else [late]
        others = [links.sibling(x) for x in [early, *ends]]
        return cat([got[0][:step], *others, got[0][step:], early, late])

    def other_half(own):
        return links.across(own.astype(bf16))

    def project(rows, cols=slice(None)):
        return jnp.dot(rows, w_in[:, cols], preferred_element_type=f32)

    def signals(rows, cols=slice(None)):
        return times_transpose(rows, w_out[cols])

    def activate(p, p_other, cols=slice(None)):
        return gelu_pair(p + p_other.astype(f32) + b_in[cols])

    def backprop(s, s_other, derivative):
        pg = ((s + s_other.astype(f32)) * derivative).astype(bf16)
        return pg, jnp.sum(pg.astype(f32), axis=0)

    tok_sib, grad_sib = links.sibling(tokens), links.sibling(out_grad)
    chunk = lambda x, y, k: cat([x[k * step : (k + 1) * step], y[k * step : (k + 1) * step]])
    toks, grads = [
        [[chunk(x, y, k)] for k in range(2)] for x, y in ((tokens, tok_sib), (out_grad, grad_sib))
    ]

    for d in range(1, far + 1):
        toks[0].append(onward(toks[0][-1], d))
        grads[0].append(onward(grads[0][-1], d))
    tok1, grad1 = rows_of(toks[0]), rows_of(grads[0])

    t, g = toks[1], grads[1]
    halves = [slice(0, w_in.shape[1] // 2), slice(w_in.shape[1] // 2, None)]
    t.append(onward(t[0], 1, toks[0][far - 1]))
    g.append(onward(g[0], 1, grads[0][far - 1]))
    p1, t[1], g[1] = pair(project(tok1), t[1], g[1])
    t.append(onward(t[1], 2))
    g.append(onward(g[1], 2))
    for d in range(3, far):
        t.append(onward(t[-1], d))
    p1x = other_half(p1)
    s_a, g[2], t[far - 1] = pair(signals(after(grad1, t[2], p1), halves[0]), g[2], t[far - 1])
    for d in range(3, far):
        g.append(onward(g[-1], d))
    t.append(onward(t[-1], far))
    s_b, g[far - 1], t[far] = pair(signals(after(grad1, s_a), halves[1]), g[far - 1], t[far])
    s_ax, s_bx = other_half(s_a), other_half(s_b)
    g.append(onward(g[-1], far))
    tok2, grad2 = rows_of(t, True), rows_of(g)
    p2, s_ax = pair(project(tok2), s_ax)
    s2 = signals(after(grad2, p2))
    act1, slope1 = activate(p1, p1x)
    pg1, sum1 = backprop(cat([s_a, s_b], axis=1), cat([s_ax, s_bx], axis=1), slope1)
    act1, pg1, sum1 = pair(act1.astype(bf16), pg1, sum1)

    def own_sums(pg, *beside):
        keep, send, *beside = pair(*back_rows(pg, w_in, w_in.shape[0] // 6), *beside)
        return send, keep + links.sibling(send).astype(f32), beside

    def scatter(own, beside):
        running = own[(2 * far - 1) * step :].astype(bf16)
        for n, d in enumerate(range(far - 1, -1, -1)):
            work = beside(n, running)
            running = links.onward(running)
            if d == 0:
                ours = own[:step] + running[step:].astype(f32)
                return (ours + links.sibling(running[:step]).astype(f32)).astype(bf16), work
            here = own[(2 * d - 1) * step : (2 * d + 1) * step]
            if n == 0:
                first = here[:step] + running.astype(f32)
                running = cat([first.astype(bf16), here[step:].astype(bf16)])
            else:
                running = (here + running.astype(f32)).astype(bf16)
            if work is not None:
                running = after(running, work)

    def pieces(x, n):
        size = x.shape[0] // n
        return [x[i * size : (i + 1) * size] for i in range(n)]

    p2_a, p2_b = pieces(p2, 2)
    s2, p2x_a = pair(s2, other_half(p2_a))
    cuts = (0, 4 * step, 10 * step, 16 * step)
    s2_first, *s2_rest = [s2[a:b] for a, b in zip(cuts, cuts[1:])]
    part1, own1, (p2x_b, *s2x) = own_sums(
        after(pg1, s2), other_half(after(p2_b, s2)), other_half(s2_first)
    )
    act2, slope2 = activate(p2, cat([p2x_a, p2x_b]))
    act2, slope2 = pair(act2.astype(bf16), slope2)
    made = {}

    def beside1(n, ready):
        if n == 2:
            pg2, made["sum2"] = backprop(s2, cat(after(s2x, ready)), slope2)
            made["pg2"] = pg2
            made["keep"], made["send"] = pair(*back_rows(pg2, w_in, w_in.shape[0] // 6))
            made["theirs"] = links.sibling(made["send"])
            return made["send"]
        wait = made.get("send", made.get("out", part1))
        a1, a2 = after((act1, act2), ready, wait)
        out = over_rows_tiles(
            [a1, a2], [grad1, grad2], made.get("out"), 2 * min(n, 2), 2, act1.shape[1] // 6
        )
        if n == 3:
            made["out"], made["theirs"] = pair(out, made["theirs"])
        else:
            made["out"], more = pair(out, other_half(after(s2_rest[n], wait)))
            s2x.append(more)
        return made["out"]

    in1, _ = scatter(own1, beside1)
    own2 = made["keep"] + made["theirs"].astype(f32)

    def beside2(n, ready):
        if n == 3:
            return None
        t1, t2 = after((tok1, tok2), ready, made.get("in", made["out"]))
        made["in"] = over_rows_tiles(
            [t1, t2], [pg1, made["pg2"]], made.get("in"), 2 * n, 2, tokens.shape[1] // 6
        )
        return made["in"]

    in2, _ = scatter(own2, beside2)
    return (cat([in1, in2]), made["in"], made["out"], sum1 + made["sum2"])


def solution(mesh):
    in_specs = (
        P(("pipe", "tensor"), "dp"),
        P(("pipe", "tensor"), "dp"),
        P("dp", ("pipe", "tensor")),
        P(("pipe", "tensor")),
        P(("pipe", "tensor"), "dp"),
    )
    out_specs = (
        P(("pipe", "tensor"), "dp"),
        P("dp", ("pipe", "tensor")),
        P(("pipe", "tensor"), "dp"),
        P(("pipe", "tensor")),
    )
    pipe, dp, tensor = (mesh.shape[a] for a in ("pipe", "dp", "tensor"))
    if dp == 2 and tensor == 4:
        links = Links(pipe, tensor)
        body = lambda *args: shards_ring(links, *args)
    else:
        body = shards_plain
    return jax.shard_map(body, mesh=mesh, in_specs=in_specs, out_specs=out_specs, check_vma=False)
```
